128 devices in a mesh: cluster: 8 (over z, x_hi), dp: 16 (over y, x_lo, core).
Axes of the slice: x: 4 (x_hi: 2, x_lo: 2; x = x_hi * 2 + x_lo), y: 4, z: 4, core: 2. Of those that a mesh axis runs over, the one named last changes fastest.
Arguments:
- documents: bfloat16 [32768, 1024], P('dp', 'cluster'), may hold values from -64 to 64
- centroids: bfloat16 [16384, 1024], P('cluster'), may hold values from -8 to 8
- domain_mass: float32 [32768, 256], P('dp'), may hold values from 0.01 to 10
Outputs:
- lift: float32 [16384, 256], P(('cluster', 'dp'))
- information: float32 [], replicated
The draws below stay inside these ranges and needn't reach their ends.
All inputs are finite; a program needn't handle non-finite values.
Results may differ from the reference program's by a relative error of at most 0.0013.
Values may be sent and summed in bfloat16 or wider, within the bound.
A program may use at most 128 MiB of HBM per device.

```python
import math
import jax
import jax.numpy as jnp
from jax import lax

E = 1024
K = 16384
G = 256
DOC_DEV = 2048
DOCS = 32768
N_DP = 16


def centroid_table(key):
    base_key = jax.random.fold_in(key, 11)
    first_key = jax.random.fold_in(base_key, 0)
    return jnp.clip(jax.random.normal(first_key, (K, E), jnp.float32), -6.0, 6.0)


def draw_centroids(key, part):
    return centroid_table(key).astype(jnp.bfloat16)


def draw_documents(key, part):
    base_key = jax.random.fold_in(key, 23)
    drawn_key = jax.random.fold_in(base_key, 0)
    pick_key = jax.random.fold_in(base_key, 2)
    drawn = jnp.clip(jax.random.normal(drawn_key, (DOCS, E), jnp.float32), -6.0, 6.0)
    table = centroid_table(key)
    positions = jnp.arange(DOCS)
    picked = 2 * jax.random.randint(pick_key, (DOCS,), 0, K // 2)
    levels = jnp.array([4.0, 6.0, 8.0, 9.5], jnp.float32)
    strength = levels[positions // 64 % 4] * (8.0 / math.sqrt(E))
    aligned = strength[:, None] * table[picked]
    chosen = jnp.where((positions % 64 == 0)[:, None], aligned, drawn)
    return chosen.astype(jnp.bfloat16)


def draw_domain_mass(key, part):
    base_key = jax.random.fold_in(key, 37)
    value_key, offset_key = jax.random.split(base_key)
    positions = jnp.arange(DOCS)[:, None]
    columns = jnp.arange(G)[None, :]
    offset = jax.random.randint(offset_key, (), 0, 16)
    favoured = columns % 16 == (positions // DOC_DEV * 5 + offset) % 16
    base = jnp.exp(jax.random.uniform(value_key, (DOCS, G), jnp.float32, math.log(0.01), 0.0))
    return jnp.where(favoured, base * 10.0, base)


def setup_inputs(seed: int = 0) -> dict:
    key_of = jax.random.split(jax.random.key(seed), 4)
    return {
        "documents": draw_documents(jax.random.fold_in(key_of[3], 71), 0),
        "centroids": draw_centroids(jax.random.fold_in(key_of[3], 71), 0),
        "domain_mass": draw_domain_mass(jax.random.fold_in(key_of[3], 71), 0),
    }


def reference(documents, centroids, domain_mass):
    scale = 3.0 / math.sqrt(E)
    shares = (domain_mass / lax.optimization_barrier(jnp.sum(domain_mass, axis=1, keepdims=True))).astype(jnp.bfloat16)
    doc_blocks = documents.reshape(N_DP, DOC_DEV, E)
    share_blocks = shares.reshape(N_DP, DOC_DEV, G)

    def accumulate(total, pair):
        block_docs, block_shares = pair
        scores = jnp.dot(block_docs, centroids.T, preferred_element_type=jnp.float32) * scale
        row_max = lax.optimization_barrier(jnp.max(scores, axis=1, keepdims=True))
        expo = jnp.exp(scores - row_max)
        row_total = lax.optimization_barrier(jnp.sum(expo, axis=1, keepdims=True))
        assign = (expo / row_total).astype(jnp.bfloat16)
        term = lax.dot_general(assign, block_shares, (((0,), (0,)), ((), ())), preferred_element_type=jnp.float32)
        return (total + term, None)
    summed, _ = lax.scan(accumulate, jnp.zeros((K, G), jnp.float32), (doc_blocks, share_blocks))
    joint = summed / DOCS
    cluster_mass = lax.optimization_barrier(jnp.sum(joint, axis=1))
    domain_prior = lax.optimization_barrier(jnp.sum(joint, axis=0))
    lift = joint / (cluster_mass[:, None] * domain_prior[None, :])
    information = jnp.sum(joint * jnp.log(lift))
    return (lift, information)
```

```python
import math

import jax
import jax.numpy as jnp
from jax import lax
from jax.experimental import pallas as pl
from jax.experimental.pallas import tpu as pltpu
from jax.sharding import PartitionSpec as P

MESH = pl.DeviceIdType.MESH
NT = (((1,), (1,)), ((), ()))

E = 1024
G = 256
DOCS = 32768
HALF = 1024
CH = 256
NJ = HALF // CH
NU = 2 * NJ
STRIPE = 128
ROWS = 1024
EXP2_SCALE = 3.0 / math.sqrt(E) * math.log2(math.e)
REL_Y = (0, 1, 3, 2)
SLOT = {rel: p for p, rel in enumerate(REL_Y)}
SETS = ((0, 1024), (1024, 768), (1792, 256))


def kernel(docs_hbm, cent_hbm, mass_hbm, lift_ref, info_ref,
           docs, own_c, far_c, mass, shares, expo, setstat, stats, acc,
           rs_out, rs_in, pr_out, pr_in, pr2_out, pr2_in, in_out, in_in, in2_out, in2_in,
           load_sem, x_send, x_recv, z_send, z_recv, f_send, f_recv, s_send, s_recv,
           b_send, b_recv, y_send, y_recv, h_send, h_recv, st_send, st_recv,
           rs_send, rs_recv, pr_send, pr_recv, pr2_send, pr2_recv, in_send, in_recv, in2_send, in2_recv):
    c = lax.axis_index("cluster")
    d = lax.axis_index("dp")
    z, xh = c // 2, lax.rem(c, 2)
    y, xl, q = d // 4, lax.rem(d // 2, 2), lax.rem(d, 2)

    def dev(dz=0, fx=0, dy=0, fl=0, fq=0):
        zz = lax.rem(z + dz, 4) if dz else z
        yy = lax.rem(y + dy, 4) if dy else y
        hh = 1 - xh if fx else xh
        ll = 1 - xl if fl else xl
        qq = 1 - q if fq else q
        return (zz * 2 + hh, (yy * 2 + ll) * 2 + qq)

    line = [(dz, fq) for fq in (0, 1) for dz in (0, 1, 2, 3) if dz or fq]
    plane = [(fx, dy, fl) for fx in (0, 1) for dy in (0, 1, 2, 3) for fl in (0, 1) if fx or dy or fl]

    def remote(src, dst, send, recv, device):
        return pltpu.make_async_remote_copy(
            src_ref=src, dst_ref=dst, send_sem=send, recv_sem=recv,
            device_id=device, device_id_type=MESH)

    barrier = pltpu.get_barrier_semaphore()
    for dz, fq in line:
        pl.semaphore_signal(barrier, inc=1, device_id=dev(dz=dz, fq=fq), device_id_type=MESH)
    for fx, dy, fl in plane:
        pl.semaphore_signal(barrier, inc=1, device_id=dev(fx=fx, dy=dy, fl=fl), device_id_type=MESH)

    def cols(cc):
        return pl.ds(pl.multiple_of(cc * 128, 128), 128)

    mine, other = cols(c), cols(z * 2 + 1 - xh)
    base = xh * HALF

    loads = [pltpu.make_async_copy(mass_hbm.at[pl.ds(pl.multiple_of(base, HALF), HALF)], mass, load_sem.at[0])]
    for j in range(NJ):
        rows = pl.ds(pl.multiple_of(base + j * CH, CH), CH)
        loads.append(pltpu.make_async_copy(docs_hbm.at[rows], docs.at[2 * j, :, mine], load_sem.at[1 + j]))
    for p in range(4):
        for fl in range(2):
            u = lax.rem(y + REL_Y[p], 4) * 2 + (1 - xl if fl else xl)
            row = pl.multiple_of(u * 256 + q * STRIPE, STRIPE)
            k = p * 2 + fl
            loads.append(pltpu.make_async_copy(
                cent_hbm.at[pl.ds(row, STRIPE)], own_c.at[pl.ds(k * STRIPE, STRIPE)], load_sem.at[1 + NJ + k]))
    for copy in loads:
        copy.start()
    loads[0].wait()
    pl.semaphore_wait(barrier, len(line) + len(plane))

    sends = []

    def go(copy):
        copy.start()
        sends.append(copy)
        return copy

    x_copies = []
    for j in range(NJ):
        rows = pl.ds(pl.multiple_of((1 - xh) * HALF + j * CH, CH), CH)
        x_copies.append(go(remote(docs_hbm.at[rows], docs.at[2 * j, :, mine], x_send.at[j], x_recv.at[j], dev(fx=1))))
    b_copies = []
    for fl in range(2):
        u = y * 2 + (xl if fl else 1 - xl)
        row = pl.multiple_of(u * 256 + q * STRIPE, STRIPE)
        b_copies.append(go(remote(
            cent_hbm.at[pl.ds(row, STRIPE)], far_c.at[pl.ds(fl * STRIPE, STRIPE)],
            b_send.at[fl], b_recv.at[fl], dev(fx=1, fl=1))))
    z_copies = []
    for j in range(NJ):
        rows = pl.ds(pl.multiple_of(base + j * CH, CH), CH)
        for dz in (1, 3, 2):
            z_copies.append(go(remote(
                docs_hbm.at[rows], docs.at[2 * j, :, mine], z_send.at[j, dz - 1], z_recv.at[j, dz - 1], dev(dz=dz))))

    for r in range(0, HALF, 256):
        block = mass[r:r + 256]
        shares[0, r:r + 256] = (block / jnp.sum(block, axis=1, keepdims=True)).astype(jnp.bfloat16)
    h_copy = go(remote(shares.at[0], shares.at[1], h_send, h_recv, dev(fq=1)))

    f_copies, y_copies = [], []

    def forward_x(j):
        x_copies[j].wait_recv()
        for dz in (1, 3, 2):
            f_copies.append(go(remote(
                docs.at[2 * j, :, other], docs.at[2 * j, :, other],
                f_send.at[j, dz - 1], f_recv.at[j, dz - 1], dev(dz=dz))))

    def forward_b(fl):
        b_copies[fl].wait_recv()
        for dy in (1, 3, 2):
            k = SLOT[4 - dy] * 2 + fl
            y_copies.append(go(remote(
                far_c.at[pl.ds(fl * STRIPE, STRIPE)], far_c.at[pl.ds(k * STRIPE, STRIPE)],
                y_send.at[fl, dy - 1], y_recv.at[fl, dy - 1], dev(dy=dy))))

    forward_x(0)
    forward_x(1)
    forward_b(0)
    forward_x(2)
    forward_x(3)
    forward_b(1)

    def part(u, s):
        start, count = SETS[s]
        block_docs = docs[u]
        top = jnp.full((8, CH), -jnp.inf, jnp.float32)
        for r in range(start, start + count, 256):
            block = own_c[r:r + 256] if r < ROWS else far_c[r - ROWS:r - ROWS + 256]
            raw = lax.dot_general(block, block_docs, NT, preferred_element_type=jnp.float32)
            expo[u, r:r + 256] = raw
            top = jnp.maximum(top, jnp.max(raw.reshape(32, 8, CH), axis=0))
        top = jnp.max(top, axis=0, keepdims=True)
        total = jnp.zeros((8, CH), jnp.float32)
        for r in range(start, start + count, 256):
            value = jnp.exp2((expo[u, r:r + 256] - top) * EXP2_SCALE)
            expo[u, r:r + 256] = value
            total = total + jnp.sum(value.reshape(32, 8, CH), axis=0)
        setstat[u, s:s + 1] = top
        setstat[u, 3 + s:4 + s] = jnp.sum(total, axis=0, keepdims=True)

    s_copies = []

    def gather_chunk(j):
        loads[1 + j].wait()
        for dz in (1, 3, 2):
            z_copies[3 * j + (1, 3, 2).index(dz)].wait_recv()
            f_copies[3 * j + (1, 3, 2).index(dz)].wait_recv()
        s_copies.append(go(remote(docs.at[2 * j], docs.at[2 * j + 1], s_send.at[j], s_recv.at[j], dev(fq=1))))

    for j in range(NJ - 1):
        gather_chunk(j)
        if j == 0:
            for copy in loads[1 + NJ:]:
                copy.wait()
        part(2 * j, 0)
        s_copies[j].wait_recv()
        part(2 * j + 1, 0)

    for i in (0, 1, 3, 4):
        y_copies[i].wait_recv()

    @pl.loop(0, NU - 2)
    def _(u):
        part(u, 1)

    gather_chunk(NJ - 1)
    part(NU - 2, 0)
    part(NU - 2, 1)
    s_copies[NJ - 1].wait_recv()
    part(NU - 1, 0)
    part(NU - 1, 1)
    for copy in y_copies[2::3]:
        copy.wait_recv()

    me = z * 2 + q

    def stat_copy(u, i):
        dz, fq = line[i]
        there = u + 1 - 2 * lax.rem(u, 2) if fq else u
        return remote(stats.at[u, me], stats.at[there, me], st_send.at[u, i], st_recv.at[there, i], dev(dz=dz, fq=fq))

    @pl.loop(0, NU)
    def _(u):
        part(u, 2)
        top3 = setstat[u, 0:3]
        top = jnp.max(top3, axis=0, keepdims=True)
        total = jnp.sum(setstat[u, 3:6] * jnp.exp2((top3 - top) * EXP2_SCALE), axis=0, keepdims=True)
        stats[u, me, 0:1] = top
        stats[u, me, 1:2] = total
        for i in range(len(line)):
            stat_copy(u, i).start()

    h_copy.wait_recv()

    @pl.loop(0, NU)
    def _(u):
        for i in range(len(line)):
            stat_copy(u, i).wait_send()
        for i in range(len(line)):
            dz, fq = line[i]
            remote(stats.at[u, me], stats.at[u, me], st_send.at[u, i], st_recv.at[u, i], dev(dz=dz, fq=fq)).wait_recv()
        tops = stats[u, :, 0, :]
        totals = stats[u, :, 1, :]
        top = jnp.max(tops, axis=0, keepdims=True)
        total = jnp.sum(totals * jnp.exp2((tops - top) * EXP2_SCALE), axis=0, keepdims=True)
        factor = jnp.exp2((setstat[u, 0:3] - top) * EXP2_SCALE) / total
        block_shares = shares[lax.rem(u, 2), pl.ds(pl.multiple_of(u // 2 * CH, CH), CH)]
        first = u == 0
        for s, (start, count) in enumerate(SETS):
            for r in range(start, start + count, 256):
                assign = (expo[u, r:r + 256] * factor[s:s + 1]).astype(jnp.bfloat16)
                term = jnp.dot(assign, block_shares, preferred_element_type=jnp.float32)
                acc[r:r + 256] = jnp.where(first, term, acc[r:r + 256] + term)

    rs_copies = []
    for k in range(1, 16):
        fx, p, fl = k // 8, k // 2 % 4, k % 2
        rows = pl.ds(k * STRIPE, STRIPE)
        rs_out[rows] = acc[rows].astype(jnp.bfloat16)
        rs_copies.append(go(remote(
            rs_out.at[rows], rs_in.at[k], rs_send.at[k], rs_recv.at[k], dev(fx=fx, dy=REL_Y[p], fl=fl))))

    here = (y * 2 + xl) * 2 + xh
    column = jnp.zeros((8, G), jnp.float32)
    for r in range(0, 2 * ROWS, 256):
        column = column + jnp.sum(acc[r:r + 256].reshape(32, 8, G), axis=0)

    def reduce_over(value, peers, index, out, box, send, recv):
        out[...] = value
        box[index] = value
        copies = [go(remote(out, box.at[index], send.at[i], recv.at[i], peer)) for i, peer in enumerate(peers)]
        return copies

    plane_devices = [dev(fx=fx, dy=dy, fl=fl) for fx, dy, fl in plane]
    line_devices = [dev(dz=dz, fq=fq) for dz, fq in line]
    copies = reduce_over(jnp.sum(column, axis=0, keepdims=True), plane_devices, here, pr_out, pr_in, pr_send, pr_recv)
    for copy in copies:
        copy.wait_recv()
    copies = reduce_over(jnp.sum(pr_in[...], axis=0), line_devices, me, pr2_out, pr2_in, pr2_send, pr2_recv)

    total = acc[0:STRIPE]
    for k, copy in enumerate(rs_copies):
        copy.wait_recv()
        total = total + rs_in[k + 1].astype(jnp.float32)
    for copy in copies:
        copy.wait_recv()
    prior = jnp.sum(pr2_in[...], axis=0) / DOCS
    joint = total / DOCS
    cluster_mass = jnp.sum(joint, axis=1, keepdims=True)
    lift = joint / (cluster_mass * prior)
    lift_ref[...] = lift
    information = jnp.sum((joint * jnp.log(lift)).reshape(STRIPE // 8, 8, G), axis=0)
    information = jnp.sum(information, axis=0, keepdims=True)

    copies = reduce_over(information, line_devices, me, in_out, in_in, in_send, in_recv)
    for copy in copies:
        copy.wait_recv()
    copies = reduce_over(jnp.sum(in_in[...], axis=0), plane_devices, here, in2_out, in2_in, in2_send, in2_recv)
    for copy in copies:
        copy.wait_recv()
    info_ref[...] = jnp.sum(jnp.sum(in2_in[...], axis=0), axis=1, keepdims=True)
    for copy in sends:
        copy.wait_send()


def shards(documents, centroids, domain_mass):
    bf16, f32 = jnp.bfloat16, jnp.float32
    dma = pltpu.SemaphoreType.DMA
    vmem = pltpu.VMEM
    lift, information = pl.pallas_call(
        kernel,
        out_shape=(jax.ShapeDtypeStruct((STRIPE, G), f32), jax.ShapeDtypeStruct((1, 1), f32)),
        in_specs=[pl.BlockSpec(memory_space=pl.ANY)] * 3,
        out_specs=(pl.BlockSpec(memory_space=pltpu.VMEM), pl.BlockSpec(memory_space=pltpu.VMEM)),
        scratch_shapes=[
            vmem((NU, CH, E), bf16),
            vmem((ROWS, E), bf16),
            vmem((ROWS, E), bf16),
            vmem((HALF, G), f32),
            vmem((2, HALF, G), bf16),
            vmem((NU, 2 * ROWS, CH), f32),
            vmem((NU, 8, CH), f32),
            vmem((NU, 8, 2, CH), f32),
            vmem((2 * ROWS, G), f32),
            vmem((2 * ROWS, G), bf16),
            vmem((16, STRIPE, G), bf16),
            vmem((1, G), f32),
            vmem((16, 1, G), f32),
            vmem((1, G), f32),
            vmem((8, 1, G), f32),
            vmem((1, G), f32),
            vmem((8, 1, G), f32),
            vmem((1, G), f32),
            vmem((16, 1, G), f32),
            dma((1 + NJ + 8,)),
            dma((NJ,)), dma((NJ,)),
            dma((NJ, 3)), dma((NJ, 3)),
            dma((NJ, 3)), dma((NJ, 3)),
            dma((NJ,)), dma((NJ,)),
            dma((2,)), dma((2,)),
            dma((2, 3)), dma((2, 3)),
            dma, dma,
            dma((NU, 7)), dma((NU, 7)),
            dma((16,)), dma((16,)),
            dma((15,)), dma((15,)),
            dma((7,)), dma((7,)),
            dma((7,)), dma((7,)),
            dma((15,)), dma((15,)),
        ],
        compiler_params=pltpu.CompilerParams(
            collective_id=0, has_side_effects=True, vmem_limit_bytes=56 << 20),
    )(documents, centroids, domain_mass)
    return lift, information.reshape(())


def solution(mesh):
    return jax.shard_map(
        shards,
        mesh=mesh,
        in_specs=(P("dp", "cluster"), P("cluster", None), P("dp", None)),
        out_specs=(P(("cluster", "dp"), None), P()),
        check_vma=False,
    )
```

```python
import math

import jax
import jax.numpy as jnp
from jax import lax
from jax.experimental import pallas as pl
from jax.experimental.pallas import tpu as pltpu
from jax.sharding import PartitionSpec as P

MESH = pl.DeviceIdType.MESH
NT = (((1,), (1,)), ((), ()))

E = 1024
G = 256
DOCS = 32768
HALF = 1024
CH = 256
NJ = HALF // CH
NB = 8
PIECE = 256 // NB
DIRECT = (0, 1, 2, 3, 4, 5, 6, 7)
WAYS = (1, 3, 2)
ZN, FN, ZW = 2, 3, 4
PRIOR_FIRST = True
SCHEDULE = (
    "x0", "b0", "z0", "x1", "b1", "z1", "x2", "b2", "z2", "x3", "b3", "z3",
    "l0", "D0,1,2,3,4,5,6,7", "l1", "L", "c0", "l2", "l3", "p0,0", "s0", "p1,0", "c1", "p2,0",
    "s1", "p3,0", "a0,4", "P0,4,1", "c2", "a4,8", "P0,4,2", "P0,4,3", "w4", "s2", "c3", "w5",
    "t0", "w6", "s3", "w7", "t1",
)
XW, BW = 4, 4
BATCHES = ((0, 6), (6, 8))
EARLY = 6
ORDER = (14, 6, 15, 7, 10, 2, 11, 3, 12, 4, 13, 5, 8, 1, 9, 0)
NU = 2 * NJ
STRIPE = 128
ROWS = 1024
EXP2_SCALE = 3.0 / math.sqrt(E) * math.log2(math.e)
REL_Y = (0, 1, 3, 2)
SLOT = {rel: p for p, rel in enumerate(REL_Y)}
SETS = ((0, 1024), (1024, 512), (1536, 256), (1792, 256))
NS = len(SETS)


def kernel(docs_hbm, cent_hbm, mass_hbm, lift_ref, info_ref,
           docs, own_c, far_c, mass, shares, expo, setstat, stats, acc,
           rs_out, rs_in, pr_out, pr_in, pr2_out, pr2_in, in_out, in_in, in2_out, in2_in,
           load_sem, x_send, x_recv, z_send, z_recv, zz_send, zz_recv, f_send, f_recv, ff_send, ff_recv, s_send, s_recv,
           b_send, b_recv, l_send, l_recv, y_send, y_recv, h_send, h_recv, st_send, st_recv,
           rs_send, rs_recv, pr_send, pr_recv, pr2_send, pr2_recv, in_send, in_recv, in2_send, in2_recv):
    c = lax.axis_index("cluster")
    d = lax.axis_index("dp")
    z, xh = c // 2, lax.rem(c, 2)
    y, xl, q = d // 4, lax.rem(d // 2, 2), lax.rem(d, 2)

    def dev(dz=0, fx=0, dy=0, fl=0, fq=0):
        zz = lax.rem(z + dz, 4) if dz else z
        yy = lax.rem(y + dy, 4) if dy else y
        hh = 1 - xh if fx else xh
        ll = 1 - xl if fl else xl
        qq = 1 - q if fq else q
        return (zz * 2 + hh, (yy * 2 + ll) * 2 + qq)

    line = [(dz, fq) for fq in (0, 1) for dz in (0, 1, 2, 3) if dz or fq]
    plane = [(fx, dy, fl) for fx in (0, 1) for dy in (0, 1, 2, 3) for fl in (0, 1) if fx or dy or fl]

    def remote(src, dst, send, recv, device):
        return pltpu.make_async_remote_copy(
            src_ref=src, dst_ref=dst, send_sem=send, recv_sem=recv,
            device_id=device, device_id_type=MESH)

    barrier = pltpu.get_barrier_semaphore()
    for dz, fq in line:
        pl.semaphore_signal(barrier, inc=1, device_id=dev(dz=dz, fq=fq), device_id_type=MESH)
    for fx, dy, fl in plane:
        pl.semaphore_signal(barrier, inc=1, device_id=dev(fx=fx, dy=dy, fl=fl), device_id_type=MESH)

    def cols(cc):
        return pl.ds(pl.multiple_of(cc * 128, 128), 128)

    mine, other = cols(c), cols(z * 2 + 1 - xh)
    base = xh * HALF

    loads = [pltpu.make_async_copy(mass_hbm.at[pl.ds(pl.multiple_of(base, HALF), HALF)], mass, load_sem.at[0])]
    for j in range(NJ):
        rows = pl.ds(pl.multiple_of(base + j * CH, CH), CH)
        loads.append(pltpu.make_async_copy(docs_hbm.at[rows], docs.at[2 * j, :, mine], load_sem.at[1 + j]))
    for p in range(4):
        for fl in range(2):
            u = lax.rem(y + REL_Y[p], 4) * 2 + (1 - xl if fl else xl)
            row = pl.multiple_of(u * 256 + q * STRIPE, STRIPE)
            k = p * 2 + fl
            loads.append(pltpu.make_async_copy(
                cent_hbm.at[pl.ds(row, STRIPE)], own_c.at[pl.ds(k * STRIPE, STRIPE)], load_sem.at[1 + NJ + k]))
    for copy in loads:
        copy.start()
    loads[0].wait()
    pl.semaphore_wait(barrier, len(line) + len(plane))

    sends = []

    def go(copy):
        copy.start()
        sends.append(copy)
        return copy

    x_copies = []
    for j in range(NJ):
        rows = pl.ds(pl.multiple_of((1 - xh) * HALF + j * CH, CH), CH)
        x_copies.append(remote(docs_hbm.at[rows], docs.at[2 * j, :, mine], x_send.at[j], x_recv.at[j], dev(fx=1)))

    def far(n, p):
        return far_c.at[pl.ds((4 * n + p) * PIECE, PIECE)]

    def cross(n, dy, sem):
        flip = n % 2
        u = lax.rem(y + dy, 4) * 2 + (xl if flip else 1 - xl)
        row = pl.multiple_of(u * 256 + q * STRIPE + n // 2 * PIECE, PIECE)
        return remote(cent_hbm.at[pl.ds(row, PIECE)], far(n, SLOT[dy]), b_send.at[sem], b_recv.at[sem], dev(fx=1, fl=1))

    b_copies = [cross(2 * i, 0, i) for i in range(NB // 2)]
    d_copies = {n: cross(n, 2, NB // 2 + n) for n in DIRECT}

    z_copies = []
    for j in range(NJ):
        rows = pl.ds(pl.multiple_of(base + j * CH, CH), CH)
        z_copies.append([remote(
            docs_hbm.at[rows], docs.at[2 * j, :, mine], z_send.at[j, i], z_recv.at[j, i], dev(dz=WAYS[i]))
            for i in range(ZN)])

    def send_z(j):
        for copy in z_copies[j]:
            go(copy)

    def send_d(*pieces):
        for n in pieces:
            go(d_copies[n])

    for copy in x_copies[:XW]:
        go(copy)
    for copy in b_copies[:BW]:
        go(copy)
    for j in range(ZW):
        send_z(j)

    for r in range(0, HALF, 256):
        block = mass[r:r + 256]
        shares[0, r:r + 256] = (block / jnp.sum(block, axis=1, keepdims=True)).astype(jnp.bfloat16)
    h_copy = go(remote(shares.at[0], shares.at[1], h_send, h_recv, dev(fq=1)))

    f_copies, y_copies, l_copies = [], {}, []
    zz_copies, ff_copies = {}, {}

    def arrive_x(j):
        x_copies[j].wait_recv()
        if j + XW < NJ:
            go(x_copies[j + XW])
        f_copies.append([go(remote(
            docs.at[2 * j, :, other], docs.at[2 * j, :, other],
            f_send.at[j, i], f_recv.at[j, i], dev(dz=WAYS[i]))) for i in range(FN)])

    def pass_on(j, copies, side, send, recv, out):
        for i in range(2):
            copies[j][i].wait_recv()
            column = cols(lax.rem(z + (3, 1)[i], 4) * 2 + side)
            part_docs = docs.at[2 * j, pl.ds(i * CH // 2, CH // 2), column]
            out[j, i] = go(remote(part_docs, part_docs, send.at[j, i], recv.at[j, i], dev(dz=(1, 3)[i])))

    def arrive_z(j):
        pass_on(j, z_copies, xh, zz_send, zz_recv, zz_copies)

    def arrive_f(j):
        pass_on(j, f_copies, 1 - xh, ff_send, ff_recv, ff_copies)

    def along_y(n):
        y_copies[n] = [go(remote(far(n, 0), far(n, SLOT[4 - dy]), y_send.at[n, dy - 1], y_recv.at[n, dy - 1], dev(dy=dy)))
                       for dy in ((1, 3) if n in DIRECT else (1, 3, 2))]

    def arrive_b(i):
        b_copies[i].wait_recv()
        if i + BW < NB // 2:
            go(b_copies[i + BW])
        l_copies.append(go(remote(far(2 * i, 0), far(2 * i + 1, 0), l_send.at[i], l_recv.at[i], dev(fl=1))))
        along_y(2 * i)

    def arrive_l(i):
        l_copies[i].wait_recv()
        along_y(2 * i + 1)

    def part(u, s):
        start, count = SETS[s] if s is not None else (0, 2 * ROWS)
        block_docs = docs[u]
        top = jnp.full((8, CH), -jnp.inf, jnp.float32)
        for r in range(start, start + count, 256):
            block = own_c[r:r + 256] if r < ROWS else far_c[r - ROWS:r - ROWS + 256]
            raw = lax.dot_general(block, block_docs, NT, preferred_element_type=jnp.float32)
            expo[u, r:r + 256] = raw
            top = jnp.maximum(top, jnp.max(raw.reshape(32, 8, CH), axis=0))
        top = jnp.max(top, axis=0, keepdims=True)
        total = jnp.zeros((8, CH), jnp.float32)
        for r in range(start, start + count, 256):
            value = jnp.exp2((expo[u, r:r + 256] - top) * EXP2_SCALE)
            expo[u, r:r + 256] = value
            total = total + jnp.sum(value.reshape(32, 8, CH), axis=0)
        total = jnp.sum(total, axis=0, keepdims=True)
        if s is None:
            setstat[u, 0:NS] = jnp.broadcast_to(top, (NS, CH))
            setstat[u, NS:2 * NS] = jnp.concatenate([total, jnp.zeros((NS - 1, CH), jnp.float32)], axis=0)
        else:
            setstat[u, s:s + 1] = top
            setstat[u, NS + s:NS + s + 1] = total

    s_copies = []

    def gather_chunk(j):
        loads[1 + j].wait()
        for i in range(2):
            if ZN == 2:
                zz_copies[j, i].wait_recv()
            if FN == 2:
                ff_copies[j, i].wait_recv()
        for copies in (z_copies[j] if ZN == 3 else []) + (f_copies[j] if FN == 3 else []):
            copies.wait_recv()
        s_copies.append(go(remote(docs.at[2 * j], docs.at[2 * j + 1], s_send.at[j], s_recv.at[j], dev(fq=1))))

    def gather_sibling(j):
        s_copies[j].wait_recv()

    def far_pieces(first, last):
        for n in range(first, last):
            for copy in y_copies[n]:
                copy.wait_recv()
            if n in DIRECT:
                d_copies[n].wait_recv()

    me = z * 2 + q

    def group_unit(u):
        return u + q * (1 - 2 * lax.rem(u, 2))

    def merge(u):
        top_set = setstat[u, 0:NS]
        top = jnp.max(top_set, axis=0, keepdims=True)
        total = jnp.sum(setstat[u, NS:2 * NS] * jnp.exp2((top_set - top) * EXP2_SCALE), axis=0, keepdims=True)
        stats[me, group_unit(u), 0:1] = top
        stats[me, group_unit(u), 1:2] = total

    st_copies = {}

    def send_stats(batch):
        first, last = BATCHES[batch]

        @pl.loop(first, last)
        def _(u):
            merge(u)
        block = stats.at[me, pl.ds(first, last - first)]
        st_copies[batch] = [go(remote(block, block, st_send.at[batch, i], st_recv.at[batch, i], dev(dz=dz, fq=fq)))
                            for i, (dz, fq) in enumerate(line)]

    def whole(u):
        part(u, None)

    def loaded():
        for copy in loads[1 + NJ:]:
            copy.wait()

    def parts(first, last, s):
        @pl.loop(first, last)
        def _(u):
            part(u, s)

    steps = {"b": arrive_b, "x": arrive_x, "z": arrive_z, "f": arrive_f, "l": arrive_l, "c": gather_chunk, "s": gather_sibling,
             "Z": send_z, "D": send_d, "L": loaded, "p": part, "P": parts, "a": far_pieces, "w": whole, "t": send_stats}
    for step in SCHEDULE:
        steps[step[0]](*[int(v) for v in step[1:].split(",") if v])

    def factors(batch):
        for copy in st_copies[batch]:
            copy.wait_recv()

        @pl.loop(*BATCHES[batch])
        def _(u):
            tops = stats[:, group_unit(u), 0, :]
            totals = stats[:, group_unit(u), 1, :]
            top = jnp.max(tops, axis=0, keepdims=True)
            total = jnp.sum(totals * jnp.exp2((tops - top) * EXP2_SCALE), axis=0, keepdims=True)
            setstat[u, 0:NS] = jnp.exp2((setstat[u, 0:NS] - top) * EXP2_SCALE) / total

    def product(k, u):
        if k < 8:
            assign = expo[u, k * STRIPE:(k + 1) * STRIPE] * setstat[u, 0:1]
        else:
            p, fl = k // 2 % 4, k % 2
            rows = []
            for i in range(fl, NB, 2):
                r = ROWS + (4 * i + p) * PIECE
                s = [n for n, (start, count) in enumerate(SETS) if start <= r < start + count][0]
                rows.append(expo[u, r:r + PIECE] * setstat[u, s:s + 1])
            assign = jnp.concatenate(rows, axis=0)
        return jnp.dot(assign.astype(jnp.bfloat16), shares[u % 2, u // 2 * CH:(u // 2 + 1) * CH],
                       preferred_element_type=jnp.float32)

    h_copy.wait_recv()
    factors(0)

    for k in range(16):
        joint = product(k, 0)
        for u in range(1, EARLY):
            joint = joint + product(k, u)
        acc[k * STRIPE:(k + 1) * STRIPE] = joint

    factors(1)

    rs_copies = {}
    column = jnp.zeros((8, G), jnp.float32)
    for k in ORDER:
        rows = pl.ds(k * STRIPE, STRIPE)
        joint = acc[rows]
        for u in range(EARLY, NU):
            joint = joint + product(k, u)
        column = column + jnp.sum(joint.reshape(STRIPE // 8, 8, G), axis=0)
        if k:
            fx, p, fl = k // 8, k // 2 % 4, k % 2
            rs_out[rows] = joint.astype(jnp.bfloat16)
            rs_copies[k] = remote(
                rs_out.at[rows], rs_in.at[k], rs_send.at[k], rs_recv.at[k], dev(fx=fx, dy=REL_Y[p], fl=fl))
            if not PRIOR_FIRST:
                go(rs_copies[k])
        else:
            acc[rows] = joint

    here = (y * 2 + xl) * 2 + xh

    def reduce_over(value, peers, index, out, box, send, recv):
        out[...] = value
        box[index] = value
        copies = [go(remote(out, box.at[index], send.at[i], recv.at[i], peer)) for i, peer in enumerate(peers)]
        return copies

    plane_devices = [dev(fx=fx, dy=dy, fl=fl) for fx, dy, fl in plane]
    line_devices = [dev(dz=dz, fq=fq) for dz, fq in line]
    column = jnp.sum(column, axis=0, keepdims=True)
    if PRIOR_FIRST:
        copies = reduce_over(column, plane_devices, here, pr_out, pr_in, pr_send, pr_recv)
        for k in ORDER:
            if k:
                go(rs_copies[k])
        for copy in copies:
            copy.wait_recv()
        copies = reduce_over(jnp.sum(pr_in[...], axis=0), line_devices, me, pr2_out, pr2_in, pr2_send, pr2_recv)
    else:
        copies = reduce_over(column, line_devices, me, pr2_out, pr2_in, pr2_send, pr2_recv)
        for copy in copies:
            copy.wait_recv()
        copies = reduce_over(jnp.sum(pr2_in[...], axis=0), plane_devices, here, pr_out, pr_in, pr_send, pr_recv)

    total = acc[0:STRIPE]
    for k in ORDER:
        if k:
            rs_copies[k].wait_recv()
            total = total + rs_in[k].astype(jnp.float32)
    for copy in copies:
        copy.wait_recv()
    prior = jnp.sum((pr2_in if PRIOR_FIRST else pr_in)[...], axis=0) / DOCS
    joint = total / DOCS
    cluster_mass = jnp.sum(joint, axis=1, keepdims=True)
    lift = joint / (cluster_mass * prior)
    lift_ref[...] = lift
    information = jnp.sum((joint * jnp.log(lift)).reshape(STRIPE // 8, 8, G), axis=0)
    information = jnp.sum(information, axis=0, keepdims=True)

    copies = reduce_over(information, line_devices, me, in_out, in_in, in_send, in_recv)
    for copy in copies:
        copy.wait_recv()
    copies = reduce_over(jnp.sum(in_in[...], axis=0), plane_devices, here, in2_out, in2_in, in2_send, in2_recv)
    for copy in copies:
        copy.wait_recv()
    info_ref[...] = jnp.sum(jnp.sum(in2_in[...], axis=0), axis=1, keepdims=True)
    for copy in sends:
        copy.wait_send()


def shards(documents, centroids, domain_mass):
    bf16, f32 = jnp.bfloat16, jnp.float32
    dma = pltpu.SemaphoreType.DMA
    vmem = pltpu.VMEM
    lift, information = pl.pallas_call(
        kernel,
        out_shape=(jax.ShapeDtypeStruct((STRIPE, G), f32), jax.ShapeDtypeStruct((1, 1), f32)),
        in_specs=[pl.BlockSpec(memory_space=pl.ANY)] * 3,
        out_specs=(pl.BlockSpec(memory_space=pltpu.VMEM), pl.BlockSpec(memory_space=pltpu.VMEM)),
        scratch_shapes=[
            vmem((NU, CH, E), bf16),
            vmem((ROWS, E), bf16),
            vmem((ROWS, E), bf16),
            vmem((HALF, G), f32),
            vmem((2, HALF, G), bf16),
            vmem((NU, 2 * ROWS, CH), f32),
            vmem((NU, 8, CH), f32),
            vmem((8, NU, 2, CH), f32),
            vmem((2 * ROWS, G), f32),
            vmem((2 * ROWS, G), bf16),
            vmem((16, STRIPE, G), bf16),
            vmem((1, G), f32),
            vmem((16, 1, G), f32),
            vmem((1, G), f32),
            vmem((8, 1, G), f32),
            vmem((1, G), f32),
            vmem((8, 1, G), f32),
            vmem((1, G), f32),
            vmem((16, 1, G), f32),
            dma((1 + NJ + 8,)),
            dma((NJ,)), dma((NJ,)),
            dma((NJ, 3)), dma((NJ, 3)), dma((NJ, 2)), dma((NJ, 2)),
            dma((NJ, 3)), dma((NJ, 3)), dma((NJ, 2)), dma((NJ, 2)),
            dma((NJ,)), dma((NJ,)),
            dma((NB // 2 + NB,)), dma((NB // 2 + NB,)),
            dma((NB // 2,)), dma((NB // 2,)),
            dma((NB, 3)), dma((NB, 3)),
            dma, dma,
            dma((2, 7)), dma((2, 7)),
            dma((16,)), dma((16,)),
            dma((15,)), dma((15,)),
            dma((7,)), dma((7,)),
            dma((7,)), dma((7,)),
            dma((15,)), dma((15,)),
        ],
        compiler_params=pltpu.CompilerParams(
            collective_id=0, has_side_effects=True, vmem_limit_bytes=56 << 20),
    )(documents, centroids, domain_mass)
    return lift, information.reshape(())


def solution(mesh):
    return jax.shard_map(
        shards,
        mesh=mesh,
        in_specs=(P("dp", "cluster"), P("cluster", None), P("dp", None)),
        out_specs=(P(("cluster", "dp"), None), P()),
        check_vma=False,
    )
```

```python
import math

import jax
import jax.numpy as jnp
from jax import lax
from jax.experimental import pallas as pl
from jax.experimental.pallas import tpu as pltpu
from jax.sharding import PartitionSpec as P

MESH = pl.DeviceIdType.MESH
NT = (((1,), (1,)), ((), ()))

E = 1024
G = 256
DOCS = 32768
HALF = 1024
CH = 256
NJ = HALF // CH
NB = 8
PIECE = 256 // NB
DIRECT = (0, 1, 2, 3, 4, 5, 6, 7)
WAYS = (1, 3, 2)
ZN, FN, ZW = 2, 3, 4
PRIOR_FIRST = True
SETTLE, EARLY_OUT, NEAR = True, True, True
SCHEDULE = (
    "x0", "b0", "D0,1,2,3,4,5,6,7", "z0", "x1", "b1", "z1", "x2", "b2", "z2", "x3", "b3",
    "z3", "l0", "l1", "L", "c0", "l2", "l3", "p0,0", "s0", "p1,0", "c1", "p2,0",
    "s1", "p3,0", "a0,4", "P0,4,1", "c2", "p4,0", "p4,1", "a4,8", "P0,4,2", "P0,4,3", "s2", "c3",
    "p4,2", "p4,3", "w5", "t0", "w6", "s3", "w7", "t1",
)
XW, BW = 4, 4
BATCHES = ((0, 6), (6, 8))
EARLY = 6
ORDER = (14, 6, 15, 7, 10, 2, 11, 3, 12, 4, 13, 5, 8, 1, 9, 0)
NU = 2 * NJ
STRIPE = 128
ROWS = 1024
EXP2_SCALE = 3.0 / math.sqrt(E) * math.log2(math.e)
REL_Y = (0, 1, 3, 2)
SLOT = {rel: p for p, rel in enumerate(REL_Y)}
SETS = ((0, 4), (4, 6), (6, 7), (7, 8))
BLOCK = 256
NS = 8


def kernel(docs_hbm, cent_hbm, mass_hbm, lift_ref, info_ref,
           docs, own_c, far_c, mass, shares, expo, setstat, stats, acc,
           rs_out, rs_in, pr_out, pr_in, pr2_out, pr2_in, in_out, in_in, in2_out, in2_in,
           load_sem, x_send, x_recv, z_send, z_recv, zz_send, zz_recv, f_send, f_recv, ff_send, ff_recv, s_send, s_recv,
           b_send, b_recv, l_send, l_recv, y_send, y_recv, h_send, h_recv, st_send, st_recv,
           rs_send, rs_recv, pr_send, pr_recv, pr2_send, pr2_recv, in_send, in_recv, in2_send, in2_recv, lift_vmem, lift_sem):
    c = lax.axis_index("cluster")
    d = lax.axis_index("dp")
    z, xh = c // 2, lax.rem(c, 2)
    y, xl, q = d // 4, lax.rem(d // 2, 2), lax.rem(d, 2)

    def dev(dz=0, fx=0, dy=0, fl=0, fq=0):
        zz = lax.rem(z + dz, 4) if dz else z
        yy = lax.rem(y + dy, 4) if dy else y
        hh = 1 - xh if fx else xh
        ll = 1 - xl if fl else xl
        qq = 1 - q if fq else q
        return (zz * 2 + hh, (yy * 2 + ll) * 2 + qq)

    line = [(dz, fq) for fq in (0, 1) for dz in (0, 1, 2, 3) if dz or fq]
    plane = [(fx, dy, fl) for fx in (0, 1) for dy in (0, 1, 2, 3) for fl in (0, 1) if fx or dy or fl]

    def remote(src, dst, send, recv, device):
        return pltpu.make_async_remote_copy(
            src_ref=src, dst_ref=dst, send_sem=send, recv_sem=recv,
            device_id=device, device_id_type=MESH)

    barrier = pltpu.get_barrier_semaphore()
    near = [dict(dz=dz, fq=fq) for dz, fq in line if not (NEAR and dz and fq)]
    near += [dict(fx=fx, dy=dy, fl=fl) for fx, dy, fl in plane if not (NEAR and dy and (fx or fl))]
    for peer in near:
        pl.semaphore_signal(barrier, inc=1, device_id=dev(**peer), device_id_type=MESH)

    def cols(cc):
        return pl.ds(pl.multiple_of(cc * 128, 128), 128)

    mine, other = cols(c), cols(z * 2 + 1 - xh)
    base = xh * HALF

    loads = [pltpu.make_async_copy(mass_hbm.at[pl.ds(pl.multiple_of(base, HALF), HALF)], mass, load_sem.at[0])]
    for j in range(NJ):
        rows = pl.ds(pl.multiple_of(base + j * CH, CH), CH)
        loads.append(pltpu.make_async_copy(docs_hbm.at[rows], docs.at[2 * j, :, mine], load_sem.at[1 + j]))
    for p in range(4):
        for fl in range(2):
            u = lax.rem(y + REL_Y[p], 4) * 2 + (1 - xl if fl else xl)
            row = pl.multiple_of(u * 256 + q * STRIPE, STRIPE)
            k = p * 2 + fl
            loads.append(pltpu.make_async_copy(
                cent_hbm.at[pl.ds(row, STRIPE)], own_c.at[pl.ds(k * STRIPE, STRIPE)], load_sem.at[1 + NJ + k]))
    for copy in loads:
        copy.start()
    loads[0].wait()
    pl.semaphore_wait(barrier, len(near))

    sends = []

    def go(copy):
        copy.start()
        sends.append(copy)
        return copy

    x_copies = []
    for j in range(NJ):
        rows = pl.ds(pl.multiple_of((1 - xh) * HALF + j * CH, CH), CH)
        x_copies.append(remote(docs_hbm.at[rows], docs.at[2 * j, :, mine], x_send.at[j], x_recv.at[j], dev(fx=1)))

    def far(n, p):
        return far_c.at[pl.ds((4 * n + p) * PIECE, PIECE)]

    def cross(n, dy, sem):
        flip = n % 2
        u = lax.rem(y + dy, 4) * 2 + (xl if flip else 1 - xl)
        row = pl.multiple_of(u * 256 + q * STRIPE + n // 2 * PIECE, PIECE)
        return remote(cent_hbm.at[pl.ds(row, PIECE)], far(n, SLOT[dy]), b_send.at[sem], b_recv.at[sem], dev(fx=1, fl=1))

    b_copies = [cross(2 * i, 0, i) for i in range(NB // 2)]
    d_copies = {n: cross(n, 2, NB // 2 + n) for n in DIRECT}

    z_copies = []
    for j in range(NJ):
        rows = pl.ds(pl.multiple_of(base + j * CH, CH), CH)
        z_copies.append([remote(
            docs_hbm.at[rows], docs.at[2 * j, :, mine], z_send.at[j, i], z_recv.at[j, i], dev(dz=WAYS[i]))
            for i in range(ZN)])

    def send_z(j):
        for copy in z_copies[j]:
            go(copy)

    def send_d(*pieces):
        for n in pieces:
            go(d_copies[n])

    for copy in x_copies[:XW]:
        go(copy)
    for copy in b_copies[:BW]:
        go(copy)
    for j in range(ZW):
        send_z(j)

    for r in range(0, HALF, 256):
        block = mass[r:r + 256]
        shares[0, r:r + 256] = (block / jnp.sum(block, axis=1, keepdims=True)).astype(jnp.bfloat16)
    h_copy = go(remote(shares.at[0], shares.at[1], h_send, h_recv, dev(fq=1)))

    f_copies, y_copies, l_copies = [], {}, []
    zz_copies, ff_copies = {}, {}

    def arrive_x(j):
        x_copies[j].wait_recv()
        if j + XW < NJ:
            go(x_copies[j + XW])
        f_copies.append([go(remote(
            docs.at[2 * j, :, other], docs.at[2 * j, :, other],
            f_send.at[j, i], f_recv.at[j, i], dev(dz=WAYS[i]))) for i in range(FN)])

    def pass_on(j, copies, side, send, recv, out):
        for i in range(2):
            copies[j][i].wait_recv()
            column = cols(lax.rem(z + (3, 1)[i], 4) * 2 + side)
            part_docs = docs.at[2 * j, pl.ds(i * CH // 2, CH // 2), column]
            out[j, i] = go(remote(part_docs, part_docs, send.at[j, i], recv.at[j, i], dev(dz=(1, 3)[i])))

    def arrive_z(j):
        pass_on(j, z_copies, xh, zz_send, zz_recv, zz_copies)

    def arrive_f(j):
        pass_on(j, f_copies, 1 - xh, ff_send, ff_recv, ff_copies)

    def along_y(n):
        y_copies[n] = [go(remote(far(n, 0), far(n, SLOT[4 - dy]), y_send.at[n, dy - 1], y_recv.at[n, dy - 1], dev(dy=dy)))
                       for dy in ((1, 3) if n in DIRECT else (1, 3, 2))]

    def arrive_b(i):
        b_copies[i].wait_recv()
        if i + BW < NB // 2:
            go(b_copies[i + BW])
        l_copies.append(go(remote(far(2 * i, 0), far(2 * i + 1, 0), l_send.at[i], l_recv.at[i], dev(fl=1))))
        along_y(2 * i)

    def arrive_l(i):
        l_copies[i].wait_recv()
        along_y(2 * i + 1)

    def part(u, s):
        block_docs = docs[u]
        for n in range(*(SETS[s] if s is not None else (0, NS))):
            r = n * BLOCK
            block = own_c[r:r + BLOCK] if r < ROWS else far_c[r - ROWS:r - ROWS + BLOCK]
            raw = lax.dot_general(block, block_docs, NT, preferred_element_type=jnp.float32)
            top = jnp.max(raw, axis=0, keepdims=True)
            value = jnp.exp2((raw - top) * EXP2_SCALE)
            expo[u, r:r + BLOCK] = value
            setstat[u, n:n + 1] = top
            setstat[u, NS + n:NS + n + 1] = jnp.sum(value, axis=0, keepdims=True)

    s_copies = []

    def gather_chunk(j):
        loads[1 + j].wait()
        for i in range(2):
            if ZN == 2:
                zz_copies[j, i].wait_recv()
            if FN == 2:
                ff_copies[j, i].wait_recv()
        for copies in (z_copies[j] if ZN == 3 else []) + (f_copies[j] if FN == 3 else []):
            copies.wait_recv()
        s_copies.append(go(remote(docs.at[2 * j], docs.at[2 * j + 1], s_send.at[j], s_recv.at[j], dev(fq=1))))

    def gather_sibling(j):
        s_copies[j].wait_recv()

    def far_pieces(first, last):
        for n in range(first, last):
            for copy in y_copies[n]:
                copy.wait_recv()
            if n in DIRECT:
                d_copies[n].wait_recv()

    me = z * 2 + q

    def group_unit(u):
        return u + q * (1 - 2 * lax.rem(u, 2))

    def merge(u):
        top_set = setstat[u, 0:NS]
        top = jnp.max(top_set, axis=0, keepdims=True)
        total = jnp.sum(setstat[u, NS:2 * NS] * jnp.exp2((top_set - top) * EXP2_SCALE), axis=0, keepdims=True)
        stats[me, group_unit(u), 0:1] = top
        stats[me, group_unit(u), 1:2] = total

    st_copies = {}

    def send_stats(batch):
        first, last = BATCHES[batch]

        @pl.loop(first, last)
        def _(u):
            merge(u)
        block = stats.at[me, pl.ds(first, last - first)]
        st_copies[batch] = [go(remote(block, block, st_send.at[batch, i], st_recv.at[batch, i], dev(dz=dz, fq=fq)))
                            for i, (dz, fq) in enumerate(line)]

    def whole(u):
        part(u, None)

    def loaded():
        for copy in loads[1 + NJ:]:
            copy.wait()

    def parts(first, last, s):
        @pl.loop(first, last)
        def _(u):
            part(u, s)

    steps = {"b": arrive_b, "x": arrive_x, "z": arrive_z, "f": arrive_f, "l": arrive_l, "c": gather_chunk, "s": gather_sibling,
             "Z": send_z, "D": send_d, "L": loaded, "p": part, "P": parts, "a": far_pieces, "w": whole, "t": send_stats}
    for step in SCHEDULE:
        steps[step[0]](*[int(v) for v in step[1:].split(",") if v])

    def factors(batch):
        for copy in st_copies[batch]:
            copy.wait_recv()

        @pl.loop(*BATCHES[batch])
        def _(u):
            tops = stats[:, group_unit(u), 0, :]
            totals = stats[:, group_unit(u), 1, :]
            top = jnp.max(tops, axis=0, keepdims=True)
            total = jnp.sum(totals * jnp.exp2((tops - top) * EXP2_SCALE), axis=0, keepdims=True)
            setstat[u, 0:NS] = jnp.exp2((setstat[u, 0:NS] - top) * EXP2_SCALE) / total

    def product(k, u):
        if k < 8:
            assign = expo[u, k * STRIPE:(k + 1) * STRIPE] * setstat[u, k // 2:k // 2 + 1]
        else:
            p, fl = k // 2 % 4, k % 2
            rows = []
            for i in range(fl, NB, 2):
                r = ROWS + (4 * i + p) * PIECE
                s = r // BLOCK
                rows.append(expo[u, r:r + PIECE] * setstat[u, s:s + 1])
            assign = jnp.concatenate(rows, axis=0)
        return jnp.dot(assign.astype(jnp.bfloat16), shares[u % 2, u // 2 * CH:(u // 2 + 1) * CH],
                       preferred_element_type=jnp.float32)

    h_copy.wait_recv()
    factors(0)

    for k in range(16):
        joint = product(k, 0)
        for u in range(1, EARLY):
            joint = joint + product(k, u)
        acc[k * STRIPE:(k + 1) * STRIPE] = joint

    factors(1)

    rs_copies = {}
    column = jnp.zeros((8, G), jnp.float32)
    for k in ORDER:
        rows = pl.ds(k * STRIPE, STRIPE)
        joint = acc[rows]
        for u in range(EARLY, NU):
            joint = joint + product(k, u)
        column = column + jnp.sum(joint.reshape(STRIPE // 8, 8, G), axis=0)
        if k:
            fx, p, fl = k // 8, k // 2 % 4, k % 2
            rs_out[rows] = joint.astype(jnp.bfloat16)
            rs_copies[k] = remote(
                rs_out.at[rows], rs_in.at[k], rs_send.at[k], rs_recv.at[k], dev(fx=fx, dy=REL_Y[p], fl=fl))
            if not PRIOR_FIRST:
                go(rs_copies[k])
        else:
            acc[rows] = joint

    here = (y * 2 + xl) * 2 + xh

    def reduce_over(value, peers, index, out, box, send, recv):
        out[...] = value
        box[index] = value
        copies = [go(remote(out, box.at[index], send.at[i], recv.at[i], peer)) for i, peer in enumerate(peers)]
        return copies

    plane_devices = [dev(fx=fx, dy=dy, fl=fl) for fx, dy, fl in plane]
    line_devices = [dev(dz=dz, fq=fq) for dz, fq in line]
    column = jnp.sum(column, axis=0, keepdims=True)
    if PRIOR_FIRST:
        copies = reduce_over(column, plane_devices, here, pr_out, pr_in, pr_send, pr_recv)
        for k in ORDER:
            if k:
                go(rs_copies[k])
        for copy in copies:
            copy.wait_recv()
        copies = reduce_over(jnp.sum(pr_in[...], axis=0), line_devices, me, pr2_out, pr2_in, pr2_send, pr2_recv)
    else:
        copies = reduce_over(column, line_devices, me, pr2_out, pr2_in, pr2_send, pr2_recv)
        for copy in copies:
            copy.wait_recv()
        copies = reduce_over(jnp.sum(pr2_in[...], axis=0), plane_devices, here, pr_out, pr_in, pr_send, pr_recv)

    def settle():
        for copy in sends:
            copy.wait_send()
        sends.clear()

    if SETTLE:
        settle()
    total = acc[0:STRIPE]
    for k in ORDER:
        if k:
            rs_copies[k].wait_recv()
            total = total + rs_in[k].astype(jnp.float32)
    for copy in copies:
        copy.wait_recv()
    prior = jnp.sum((pr2_in if PRIOR_FIRST else pr_in)[...], axis=0) / DOCS
    joint = total / DOCS
    cluster_mass = jnp.sum(joint, axis=1, keepdims=True)
    lift = joint / (cluster_mass * prior)
    if EARLY_OUT:
        lift_vmem[...] = lift
        lift_copy = pltpu.make_async_copy(lift_vmem, lift_ref, lift_sem)
        lift_copy.start()
    else:
        lift_ref[...] = lift
    information = jnp.sum((joint * jnp.log(lift)).reshape(STRIPE // 8, 8, G), axis=0)
    information = jnp.sum(information, axis=0, keepdims=True)

    copies = reduce_over(information, line_devices, me, in_out, in_in, in_send, in_recv)
    for copy in copies:
        copy.wait_recv()
    copies = reduce_over(jnp.sum(in_in[...], axis=0), plane_devices, here, in2_out, in2_in, in2_send, in2_recv)
    for copy in copies:
        copy.wait_recv()
    info_ref[...] = jnp.sum(jnp.sum(in2_in[...], axis=0), axis=1, keepdims=True)
    settle()
    if EARLY_OUT:
        lift_copy.wait()


def shards(documents, centroids, domain_mass):
    bf16, f32 = jnp.bfloat16, jnp.float32
    dma = pltpu.SemaphoreType.DMA
    vmem = pltpu.VMEM
    lift, information = pl.pallas_call(
        kernel,
        out_shape=(jax.ShapeDtypeStruct((STRIPE, G), f32), jax.ShapeDtypeStruct((1, 1), f32)),
        in_specs=[pl.BlockSpec(memory_space=pl.ANY)] * 3,
        out_specs=(pl.BlockSpec(memory_space=pl.ANY if EARLY_OUT else pltpu.VMEM), pl.BlockSpec(memory_space=pltpu.VMEM)),
        scratch_shapes=[
            vmem((NU, CH, E), bf16),
            vmem((ROWS, E), bf16),
            vmem((ROWS, E), bf16),
            vmem((HALF, G), f32),
            vmem((2, HALF, G), bf16),
            vmem((NU, 2 * ROWS, CH), f32),
            vmem((NU, 2 * NS, CH), f32),
            vmem((8, NU, 2, CH), f32),
            vmem((2 * ROWS, G), f32),
            vmem((2 * ROWS, G), bf16),
            vmem((16, STRIPE, G), bf16),
            vmem((1, G), f32),
            vmem((16, 1, G), f32),
            vmem((1, G), f32),
            vmem((8, 1, G), f32),
            vmem((1, G), f32),
            vmem((8, 1, G), f32),
            vmem((1, G), f32),
            vmem((16, 1, G), f32),
            dma((1 + NJ + 8,)),
            dma((NJ,)), dma((NJ,)),
            dma((NJ, 3)), dma((NJ, 3)), dma((NJ, 2)), dma((NJ, 2)),
            dma((NJ, 3)), dma((NJ, 3)), dma((NJ, 2)), dma((NJ, 2)),
            dma((NJ,)), dma((NJ,)),
            dma((NB // 2 + NB,)), dma((NB // 2 + NB,)),
            dma((NB // 2,)), dma((NB // 2,)),
            dma((NB, 3)), dma((NB, 3)),
            dma, dma,
            dma((2, 7)), dma((2, 7)),
            dma((16,)), dma((16,)),
            dma((15,)), dma((15,)),
            dma((7,)), dma((7,)),
            dma((7,)), dma((7,)),
            dma((15,)), dma((15,)),
            vmem((STRIPE, G), f32),
            dma,
        ],
        compiler_params=pltpu.CompilerParams(
            collective_id=0, has_side_effects=True, vmem_limit_bytes=56 << 20),
    )(documents, centroids, domain_mass)
    return lift, information.reshape(())


def solution(mesh):
    return jax.shard_map(
        shards,
        mesh=mesh,
        in_specs=(P("dp", "cluster"), P("cluster", None), P("dp", None)),
        out_specs=(P(("cluster", "dp"), None), P()),
        check_vma=False,
    )
```

```python
import math

import jax
import jax.numpy as jnp
from jax import lax
from jax.experimental import pallas as pl
from jax.experimental.pallas import tpu as pltpu
from jax.sharding import PartitionSpec as P

MESH = pl.DeviceIdType.MESH
NT = (((1,), (1,)), ((), ()))

E = 1024
G = 256
DOCS = 32768
HALF = 1024
CH = 256
NJ = HALF // CH
NB = 8
PIECE = 256 // NB
DIRECT = (0, 1, 2, 3, 4, 5, 6, 7)
WAYS = (1, 3, 2)
ZN, FN, ZW = 2, 3, 4
PRIOR_FIRST = True
SETTLE, EARLY_OUT, NEAR = True, True, True
SCHEDULE = (
    "D0,1,2,3,4,5,6,7", "x0", "b0", "z0", "x1", "b1", "z1", "x2", "b2", "z2", "x3", "b3",
    "z3", "l0", "l1", "L", "c0", "l2", "l3", "p0,0", "s0", "p1,0", "c1", "p2,0",
    "s1", "p3,0", "a0,4", "P0,4,1", "c2", "p4,0", "p4,1", "a4,8", "P0,4,2", "P0,4,3", "s2", "c3",
    "p4,2", "p4,3", "w5", "t0", "w6", "s3", "w7", "t1",
)
XW, BW = 4, 4
BATCHES = ((0, 6), (6, 8))
EARLY = 6
ORDER = (14, 6, 15, 7, 10, 2, 11, 3, 12, 4, 13, 5, 8, 1, 9, 0)
NU = 2 * NJ
STRIPE = 128
ROWS = 1024
EXP2_SCALE = 3.0 / math.sqrt(E) * math.log2(math.e)
REL_Y = (0, 1, 3, 2)
SLOT = {rel: p for p, rel in enumerate(REL_Y)}
SETS = ((0, 4), (4, 6), (6, 7), (7, 8))
BLOCK = 256
NS = 8


def kernel(docs_hbm, cent_hbm, mass_hbm, lift_ref, info_ref,
           docs, own_c, far_c, mass, shares, expo, setstat, stats, acc,
           rs_out, rs_in, pr_out, pr_in, pr2_out, pr2_in, in_out, in_in, in2_out, in2_in,
           load_sem, x_send, x_recv, z_send, z_recv, zz_send, zz_recv, f_send, f_recv, ff_send, ff_recv, s_send, s_recv,
           b_send, b_recv, l_send, l_recv, y_send, y_recv, h_send, h_recv, st_send, st_recv,
           rs_send, rs_recv, pr_send, pr_recv, pr2_send, pr2_recv, in_send, in_recv, in2_send, in2_recv, lift_vmem, lift_sem):
    c = lax.axis_index("cluster")
    d = lax.axis_index("dp")
    z, xh = c // 2, lax.rem(c, 2)
    y, xl, q = d // 4, lax.rem(d // 2, 2), lax.rem(d, 2)

    def dev(dz=0, fx=0, dy=0, fl=0, fq=0):
        zz = lax.rem(z + dz, 4) if dz else z
        yy = lax.rem(y + dy, 4) if dy else y
        hh = 1 - xh if fx else xh
        ll = 1 - xl if fl else xl
        qq = 1 - q if fq else q
        return (zz * 2 + hh, (yy * 2 + ll) * 2 + qq)

    line = [(dz, fq) for fq in (0, 1) for dz in (0, 1, 2, 3) if dz or fq]
    plane = [(fx, dy, fl) for fx in (0, 1) for dy in (0, 1, 2, 3) for fl in (0, 1) if fx or dy or fl]

    def remote(src, dst, send, recv, device):
        return pltpu.make_async_remote_copy(
            src_ref=src, dst_ref=dst, send_sem=send, recv_sem=recv,
            device_id=device, device_id_type=MESH)

    barrier = pltpu.get_barrier_semaphore()
    near = [dict(dz=dz, fq=fq) for dz, fq in line if not (NEAR and dz and fq)]
    near += [dict(fx=fx, dy=dy, fl=fl) for fx, dy, fl in plane if not (NEAR and dy and (fx or fl))]
    for peer in near:
        pl.semaphore_signal(barrier, inc=1, device_id=dev(**peer), device_id_type=MESH)

    def cols(cc):
        return pl.ds(pl.multiple_of(cc * 128, 128), 128)

    mine, other = cols(c), cols(z * 2 + 1 - xh)
    base = xh * HALF

    loads = [pltpu.make_async_copy(mass_hbm.at[pl.ds(pl.multiple_of(base, HALF), HALF)], mass, load_sem.at[0])]
    for j in range(NJ):
        rows = pl.ds(pl.multiple_of(base + j * CH, CH), CH)
        loads.append(pltpu.make_async_copy(docs_hbm.at[rows], docs.at[2 * j, :, mine], load_sem.at[1 + j]))
    for p in range(4):
        for fl in range(2):
            u = lax.rem(y + REL_Y[p], 4) * 2 + (1 - xl if fl else xl)
            row = pl.multiple_of(u * 256 + q * STRIPE, STRIPE)
            k = p * 2 + fl
            loads.append(pltpu.make_async_copy(
                cent_hbm.at[pl.ds(row, STRIPE)], own_c.at[pl.ds(k * STRIPE, STRIPE)], load_sem.at[1 + NJ + k]))
    for copy in loads:
        copy.start()
    loads[0].wait()
    pl.semaphore_wait(barrier, len(near))

    sends = []

    def go(copy):
        copy.start()
        sends.append(copy)
        return copy

    x_copies = []
    for j in range(NJ):
        rows = pl.ds(pl.multiple_of((1 - xh) * HALF + j * CH, CH), CH)
        x_copies.append(remote(docs_hbm.at[rows], docs.at[2 * j, :, mine], x_send.at[j], x_recv.at[j], dev(fx=1)))

    def far(n, p):
        return far_c.at[pl.ds((4 * n + p) * PIECE, PIECE)]

    def cross(n, dy, sem):
        flip = n % 2
        u = lax.rem(y + dy, 4) * 2 + (xl if flip else 1 - xl)
        row = pl.multiple_of(u * 256 + q * STRIPE + n // 2 * PIECE, PIECE)
        return remote(cent_hbm.at[pl.ds(row, PIECE)], far(n, SLOT[dy]), b_send.at[sem], b_recv.at[sem], dev(fx=1, fl=1))

    b_copies = [cross(2 * i, 0, i) for i in range(NB // 2)]
    d_copies = {n: cross(n, 2, NB // 2 + n) for n in DIRECT}

    z_copies = []
    for j in range(NJ):
        rows = pl.ds(pl.multiple_of(base + j * CH, CH), CH)
        z_copies.append([remote(
            docs_hbm.at[rows], docs.at[2 * j, :, mine], z_send.at[j, i], z_recv.at[j, i], dev(dz=WAYS[i]))
            for i in range(ZN)])

    def send_z(j):
        for copy in z_copies[j]:
            go(copy)

    def send_d(*pieces):
        for n in pieces:
            go(d_copies[n])

    for copy in x_copies[:XW]:
        go(copy)
    for copy in b_copies[:BW]:
        go(copy)
    for j in range(ZW):
        send_z(j)

    for r in range(0, HALF, 256):
        block = mass[r:r + 256]
        shares[0, r:r + 256] = (block / jnp.sum(block, axis=1, keepdims=True)).astype(jnp.bfloat16)
    h_copy = go(remote(shares.at[0], shares.at[1], h_send, h_recv, dev(fq=1)))

    f_copies, y_copies, l_copies = [], {}, []
    zz_copies, ff_copies = {}, {}

    def arrive_x(j):
        x_copies[j].wait_recv()
        if j + XW < NJ:
            go(x_copies[j + XW])
        f_copies.append([go(remote(
            docs.at[2 * j, :, other], docs.at[2 * j, :, other],
            f_send.at[j, i], f_recv.at[j, i], dev(dz=WAYS[i]))) for i in range(FN)])

    def pass_on(j, copies, side, send, recv, out):
        for i in range(2):
            copies[j][i].wait_recv()
            column = cols(lax.rem(z + (3, 1)[i], 4) * 2 + side)
            part_docs = docs.at[2 * j, pl.ds(i * CH // 2, CH // 2), column]
            out[j, i] = go(remote(part_docs, part_docs, send.at[j, i], recv.at[j, i], dev(dz=(1, 3)[i])))

    def arrive_z(j):
        pass_on(j, z_copies, xh, zz_send, zz_recv, zz_copies)

    def arrive_f(j):
        pass_on(j, f_copies, 1 - xh, ff_send, ff_recv, ff_copies)

    def along_y(n):
        y_copies[n] = [go(remote(far(n, 0), far(n, SLOT[4 - dy]), y_send.at[n, dy - 1], y_recv.at[n, dy - 1], dev(dy=dy)))
                       for dy in ((1, 3) if n in DIRECT else (1, 3, 2))]

    def arrive_b(i):
        b_copies[i].wait_recv()
        if i + BW < NB // 2:
            go(b_copies[i + BW])
        l_copies.append(go(remote(far(2 * i, 0), far(2 * i + 1, 0), l_send.at[i], l_recv.at[i], dev(fl=1))))
        along_y(2 * i)

    def arrive_l(i):
        l_copies[i].wait_recv()
        along_y(2 * i + 1)

    def part(u, s):
        block_docs = docs[u]
        for n in range(*(SETS[s] if s is not None else (0, NS))):
            r = n * BLOCK
            block = own_c[r:r + BLOCK] if r < ROWS else far_c[r - ROWS:r - ROWS + BLOCK]
            raw = lax.dot_general(block, block_docs, NT, preferred_element_type=jnp.float32)
            top = jnp.max(raw, axis=0, keepdims=True)
            value = jnp.exp2((raw - top) * EXP2_SCALE)
            expo[u, r:r + BLOCK] = value
            setstat[u, n:n + 1] = top
            setstat[u, NS + n:NS + n + 1] = jnp.sum(value, axis=0, keepdims=True)

    s_copies = []

    def gather_chunk(j):
        loads[1 + j].wait()
        for i in range(2):
            if ZN == 2:
                zz_copies[j, i].wait_recv()
            if FN == 2:
                ff_copies[j, i].wait_recv()
        for copies in (z_copies[j] if ZN == 3 else []) + (f_copies[j] if FN == 3 else []):
            copies.wait_recv()
        s_copies.append(go(remote(docs.at[2 * j], docs.at[2 * j + 1], s_send.at[j], s_recv.at[j], dev(fq=1))))

    def gather_sibling(j):
        s_copies[j].wait_recv()

    def far_pieces(first, last):
        for n in range(first, last):
            for copy in y_copies[n]:
                copy.wait_recv()
            if n in DIRECT:
                d_copies[n].wait_recv()

    me = z * 2 + q

    def group_unit(u):
        return u + q * (1 - 2 * lax.rem(u, 2))

    def merge(u):
        top_set = setstat[u, 0:NS]
        top = jnp.max(top_set, axis=0, keepdims=True)
        total = jnp.sum(setstat[u, NS:2 * NS] * jnp.exp2((top_set - top) * EXP2_SCALE), axis=0, keepdims=True)
        stats[me, group_unit(u), 0:1] = top
        stats[me, group_unit(u), 1:2] = total

    st_copies = {}

    def send_stats(batch):
        first, last = BATCHES[batch]

        @pl.loop(first, last)
        def _(u):
            merge(u)
        block = stats.at[me, pl.ds(first, last - first)]
        st_copies[batch] = [go(remote(block, block, st_send.at[batch, i], st_recv.at[batch, i], dev(dz=dz, fq=fq)))
                            for i, (dz, fq) in enumerate(line)]

    def whole(u):
        part(u, None)

    def loaded():
        for copy in loads[1 + NJ:]:
            copy.wait()

    def parts(first, last, s):
        @pl.loop(first, last)
        def _(u):
            part(u, s)

    steps = {"b": arrive_b, "x": arrive_x, "z": arrive_z, "f": arrive_f, "l": arrive_l, "c": gather_chunk, "s": gather_sibling,
             "Z": send_z, "D": send_d, "L": loaded, "p": part, "P": parts, "a": far_pieces, "w": whole, "t": send_stats}
    for step in SCHEDULE:
        steps[step[0]](*[int(v) for v in step[1:].split(",") if v])

    def factors(batch):
        for copy in st_copies[batch]:
            copy.wait_recv()

        @pl.loop(*BATCHES[batch])
        def _(u):
            tops = stats[:, group_unit(u), 0, :]
            totals = stats[:, group_unit(u), 1, :]
            top = jnp.max(tops, axis=0, keepdims=True)
            total = jnp.sum(totals * jnp.exp2((tops - top) * EXP2_SCALE), axis=0, keepdims=True)
            setstat[u, 0:NS] = jnp.exp2((setstat[u, 0:NS] - top) * EXP2_SCALE) / total

    def assigned(k, u):
        if k < 8:
            return (expo[u, k * STRIPE:(k + 1) * STRIPE] * setstat[u, k // 2:k // 2 + 1]).astype(jnp.bfloat16)
        p, fl = k // 2 % 4, k % 2
        rows = []
        for i in range(fl, NB, 2):
            r = ROWS + (4 * i + p) * PIECE
            rows.append(expo[u, r:r + PIECE] * setstat[u, r // BLOCK:r // BLOCK + 1])
        return jnp.concatenate(rows, axis=0).astype(jnp.bfloat16)

    def product(k, first, last):
        total = None
        for side in range(2):
            assign = jnp.concatenate([assigned(k, u) for u in range(first + side, last, 2)], axis=1)
            term = jnp.dot(assign, shares[side, first // 2 * CH:last // 2 * CH], preferred_element_type=jnp.float32)
            total = term if total is None else total + term
        return total

    h_copy.wait_recv()
    factors(0)

    for k in range(16):
        acc[k * STRIPE:(k + 1) * STRIPE] = product(k, 0, EARLY)

    factors(1)

    rs_copies = {}
    column = jnp.zeros((8, G), jnp.float32)
    for k in ORDER:
        rows = pl.ds(k * STRIPE, STRIPE)
        joint = acc[rows] + product(k, EARLY, NU)
        column = column + jnp.sum(joint.reshape(STRIPE // 8, 8, G), axis=0)
        if k:
            fx, p, fl = k // 8, k // 2 % 4, k % 2
            rs_out[rows] = joint.astype(jnp.bfloat16)
            rs_copies[k] = remote(
                rs_out.at[rows], rs_in.at[k], rs_send.at[k], rs_recv.at[k], dev(fx=fx, dy=REL_Y[p], fl=fl))
            if not PRIOR_FIRST:
                go(rs_copies[k])
        else:
            acc[rows] = joint

    here = (y * 2 + xl) * 2 + xh

    def reduce_over(value, peers, index, out, box, send, recv):
        out[...] = value
        box[index] = value
        copies = [go(remote(out, box.at[index], send.at[i], recv.at[i], peer)) for i, peer in enumerate(peers)]
        return copies

    plane_devices = [dev(fx=fx, dy=dy, fl=fl) for fx, dy, fl in plane]
    line_devices = [dev(dz=dz, fq=fq) for dz, fq in line]
    column = jnp.sum(column, axis=0, keepdims=True)
    if PRIOR_FIRST:
        copies = reduce_over(column, plane_devices, here, pr_out, pr_in, pr_send, pr_recv)
        for k in ORDER:
            if k:
                go(rs_copies[k])
        for copy in copies:
            copy.wait_recv()
        copies = reduce_over(jnp.sum(pr_in[...], axis=0), line_devices, me, pr2_out, pr2_in, pr2_send, pr2_recv)
    else:
        copies = reduce_over(column, line_devices, me, pr2_out, pr2_in, pr2_send, pr2_recv)
        for copy in copies:
            copy.wait_recv()
        copies = reduce_over(jnp.sum(pr2_in[...], axis=0), plane_devices, here, pr_out, pr_in, pr_send, pr_recv)

    def settle():
        for copy in sends:
            copy.wait_send()
        sends.clear()

    if SETTLE:
        settle()
    total = acc[0:STRIPE]
    for k in ORDER:
        if k:
            rs_copies[k].wait_recv()
            total = total + rs_in[k].astype(jnp.float32)
    for copy in copies:
        copy.wait_recv()
    prior = jnp.sum((pr2_in if PRIOR_FIRST else pr_in)[...], axis=0) / DOCS
    joint = total / DOCS
    cluster_mass = jnp.sum(joint, axis=1, keepdims=True)
    lift = joint / (cluster_mass * prior)
    if EARLY_OUT:
        lift_vmem[...] = lift
        lift_copy = pltpu.make_async_copy(lift_vmem, lift_ref, lift_sem)
        lift_copy.start()
    else:
        lift_ref[...] = lift
    information = jnp.sum((joint * jnp.log(lift)).reshape(STRIPE // 8, 8, G), axis=0)
    information = jnp.sum(information, axis=0, keepdims=True)

    copies = reduce_over(information, line_devices, me, in_out, in_in, in_send, in_recv)
    for copy in copies:
        copy.wait_recv()
    copies = reduce_over(jnp.sum(in_in[...], axis=0), plane_devices, here, in2_out, in2_in, in2_send, in2_recv)
    for copy in copies:
        copy.wait_recv()
    info_ref[...] = jnp.sum(jnp.sum(in2_in[...], axis=0), axis=1, keepdims=True)
    settle()
    if EARLY_OUT:
        lift_copy.wait()


def shards(documents, centroids, domain_mass):
    bf16, f32 = jnp.bfloat16, jnp.float32
    dma = pltpu.SemaphoreType.DMA
    vmem = pltpu.VMEM
    lift, information = pl.pallas_call(
        kernel,
        out_shape=(jax.ShapeDtypeStruct((STRIPE, G), f32), jax.ShapeDtypeStruct((1, 1), f32)),
        in_specs=[pl.BlockSpec(memory_space=pl.ANY)] * 3,
        out_specs=(pl.BlockSpec(memory_space=pl.ANY if EARLY_OUT else pltpu.VMEM), pl.BlockSpec(memory_space=pltpu.VMEM)),
        scratch_shapes=[
            vmem((NU, CH, E), bf16),
            vmem((ROWS, E), bf16),
            vmem((ROWS, E), bf16),
            vmem((HALF, G), f32),
            vmem((2, HALF, G), bf16),
            vmem((NU, 2 * ROWS, CH), f32),
            vmem((NU, 2 * NS, CH), f32),
            vmem((8, NU, 2, CH), f32),
            vmem((2 * ROWS, G), f32),
            vmem((2 * ROWS, G), bf16),
            vmem((16, STRIPE, G), bf16),
            vmem((1, G), f32),
            vmem((16, 1, G), f32),
            vmem((1, G), f32),
            vmem((8, 1, G), f32),
            vmem((1, G), f32),
            vmem((8, 1, G), f32),
            vmem((1, G), f32),
            vmem((16, 1, G), f32),
            dma((1 + NJ + 8,)),
            dma((NJ,)), dma((NJ,)),
            dma((NJ, 3)), dma((NJ, 3)), dma((NJ, 2)), dma((NJ, 2)),
            dma((NJ, 3)), dma((NJ, 3)), dma((NJ, 2)), dma((NJ, 2)),
            dma((NJ,)), dma((NJ,)),
            dma((NB // 2 + NB,)), dma((NB // 2 + NB,)),
            dma((NB // 2,)), dma((NB // 2,)),
            dma((NB, 3)), dma((NB, 3)),
            dma, dma,
            dma((2, 7)), dma((2, 7)),
            dma((16,)), dma((16,)),
            dma((15,)), dma((15,)),
            dma((7,)), dma((7,)),
            dma((7,)), dma((7,)),
            dma((15,)), dma((15,)),
            vmem((STRIPE, G), f32),
            dma,
        ],
        compiler_params=pltpu.CompilerParams(
            collective_id=0, has_side_effects=True, vmem_limit_bytes=56 << 20),
    )(documents, centroids, domain_mass)
    return lift, information.reshape(())


def solution(mesh):
    return jax.shard_map(
        shards,
        mesh=mesh,
        in_specs=(P("dp", "cluster"), P("cluster", None), P("dp", None)),
        out_specs=(P(("cluster", "dp"), None), P()),
        check_vma=False,
    )
```
